32 devices in a mesh: groups: 2 (over y), col: 4 (over x, core), row: 4 (over z).
Axes of the slice: x: 2, y: 2, z: 4, core: 2. Of those that a mesh axis runs over, the one named last changes fastest.
Arguments:
- object_field: float32 [2, 3072, 1536], P(None, ('groups', 'row'), 'col'), parts along dimension 1, may hold values from -7 to 7
- probe: float32 [2, 4, 256, 256], P(None, 'groups'), parts along dimension 1, may hold values from -2 to 2
- positions: int32 [8, 4, 2, 8], P(('groups', 'row'), 'col'), parts along dimension 0, may hold values from 0 to 383
- counts: int32 [8, 4], P(('groups', 'row'), 'col'), parts along dimension 0, may hold values from 1 to 8, as said below
- patterns: bfloat16 [8, 4, 8, 256, 256], P(('groups', 'row'), 'col'), parts along dimension 0, may hold values from 0 to 1
Outputs:
- object_grad: float32 [2, 3072, 1536], P(None, ('groups', 'row'), 'col'), parts along dimension 1
- probe_grad: float32 [2, 4, 256, 256], P(None, 'groups'), parts along dimension 1
The draws below stay inside these ranges and needn't reach their ends.
There are 2 independent parts, one for each index of `groups`. The reference program is written for one: setup_inputs(seed, part) draws one part's arguments, and reference() takes and returns one part's arrays. A program takes and returns all parts, laid end to end along the dimension named above; each array names one. Nothing has to cross between parts.
Inputs may be any that keep to these rules, and one draw needn't show every extreme that they name: `counts`: at least one tile holds 8 live positions in every draw.
All inputs are finite; a program needn't handle non-finite values.
Results may differ from the reference program's by a relative error of at most 0.005.
Values sent between devices are 32-bit elements; how exact they have to be, the bound alone decides.
No kernel may reach another device: no remote copies, remote signals or barrier semaphores. Data moves between devices by JAX's collectives and lax.ppermute only.
A program may use at most 64 MiB of HBM per device.

```python
import math
import jax
import jax.numpy as jnp
from jax import lax

W = 256
MODES = 2
TS = 384
KMAX = 8
NY = 1536
NX = 1536


def draw_counts(key, part):
    key = jax.random.fold_in(key, 11)
    first_key, second_key, third_key = jax.random.split(key, 3)
    tile_rows = NY // TS
    tile_cols = NX // TS
    factor_one = jax.random.randint(first_key, (tile_rows, tile_cols), 0, KMAX, dtype=jnp.int32)
    factor_two = jax.random.randint(second_key, (tile_rows, tile_cols), 0, KMAX, dtype=jnp.int32)
    loads = (1 + factor_one * factor_two // KMAX).reshape(-1)
    chosen = jax.random.randint(third_key, (), 0, tile_rows * tile_cols, dtype=jnp.int32)
    loads = jnp.where(jnp.arange(tile_rows * tile_cols, dtype=jnp.int32) == chosen, KMAX, loads)
    return loads.reshape(tile_rows, tile_cols).astype(jnp.int32)


def draw_object_field(key, part):
    key = jax.random.fold_in(key, 23)
    first_key = jax.random.fold_in(key, 0)
    rows_frac = jnp.arange(NY, dtype=jnp.float32) / NY
    cols_frac = jnp.arange(NX, dtype=jnp.float32) / NX
    envelope = jnp.sqrt(1.0 + rows_frac[:, None] + cols_frac[None, :])
    values = jnp.clip(jax.random.normal(first_key, (2, NY, NX), jnp.float32), -4.0, 4.0)
    return (values * envelope[None]).astype(jnp.float32)


def plant(array, rng, low, largest):
    index_at = [jax.random.randint(jax.random.fold_in(rng, axis), (), 0, length) for axis, length in enumerate(array.shape)]
    widest = array.shape.index(max(array.shape))
    beside = index_at[:widest] + [(index_at[widest] + 1) % array.shape[widest]] + index_at[widest + 1:]
    return array.at[tuple(index_at)].set(low).at[tuple(beside)].set(largest)


def shard_levels(rng, dims, shards, least, top_value):
    gain = 1.0
    for position, parts in shards:
        heights = jax.random.uniform(jax.random.fold_in(jax.random.fold_in(rng, 6), position), (parts,), jnp.float32, least / len(shards), top_value / len(shards))
        gain = gain * jnp.repeat(jnp.exp(heights), dims[position] // parts).reshape((-1,) + (1,) * (len(dims) - 1 - position))
    return gain


def gaussian(key, extent, deviation, most, kind=jnp.bfloat16):
    result = jax.random.normal(key, extent, jnp.float32) * deviation
    return jnp.minimum(jnp.maximum(result, -most), most).astype(kind)


def setup_inputs(seed: int = 0, part: int = 0) -> dict:
    key_of = jax.random.split(jax.random.key(seed), 6)
    own_keys = jax.random.split(jax.random.fold_in(key_of[5], part), 6)
    return {
        "object_field": draw_object_field(jax.random.fold_in(jax.random.fold_in(key_of[5], part), 71), part),
        "probe": gaussian(own_keys[1], (2, MODES, W, W), 0.35, 2.0, jnp.float32),
        "positions": plant(jax.random.randint(own_keys[2], (NY // TS, NX // TS, 2, KMAX), 0, TS), jax.random.fold_in(own_keys[2], 1), 0, TS - 1).astype(jnp.int32),
        "counts": draw_counts(jax.random.fold_in(jax.random.fold_in(key_of[5], part), 71), part),
        "patterns": jnp.clip(1.0 * jax.random.uniform(own_keys[4], (NY // TS, NX // TS, KMAX, W, W), jnp.float32) ** shard_levels(own_keys[4], (NY // TS, NX // TS, KMAX, W, W), ((0, 4), (1, 4)), -0.2, 0.2), 0.0, 1.0).astype(jnp.bfloat16),
    }


def dft_tables():
    counter = jnp.arange(W, dtype=jnp.int32)
    phases = counter[:, None] * counter[None, :] % W
    angles = 2.0 * math.pi / W * phases.astype(jnp.float32)
    scaling = 1.0 / math.sqrt(W)
    return ((jnp.cos(angles) * scaling).astype(jnp.bfloat16), (jnp.sin(angles) * scaling).astype(jnp.bfloat16))

def right_factor(cosine_table, sine_table, direction):
    upper = jnp.concatenate([cosine_table, -direction * sine_table], axis=1)
    lower = jnp.concatenate([direction * sine_table, cosine_table], axis=1)
    return jnp.concatenate([upper, lower], axis=0)

def transform(wavefield, cosine_table, sine_table, direction):
    factor = right_factor(cosine_table, sine_table, direction).astype(jnp.float32)
    halfway = jnp.einsum('bjx,xy->bjy', wavefield.astype(jnp.float32), factor).astype(jnp.bfloat16)
    with_cosine = jnp.einsum('jk,bkx->bjx', cosine_table.astype(jnp.float32), halfway.astype(jnp.float32))
    with_sine = jnp.einsum('jk,bkx->bjx', sine_table.astype(jnp.float32), halfway.astype(jnp.float32))
    real_part = with_cosine[..., :W] + direction * with_sine[..., W:]
    imag_part = with_cosine[..., W:] - direction * with_sine[..., :W]
    return (real_part, imag_part)

def reference(object_field, probe, positions, counts, patterns):
    margin = W // 2
    tile_rows = NY // TS
    tile_cols = NX // TS
    cosine_table, sine_table = dft_tables()
    padded = jnp.pad(object_field, ((0, 0), (margin, margin), (margin, margin)))
    row_start = (jnp.arange(tile_rows, dtype=jnp.int32)[:, None, None] * TS + positions[:, :, 0, :]).reshape(-1).astype(jnp.int32)
    col_start = (jnp.arange(tile_cols, dtype=jnp.int32)[None, :, None] * TS + positions[:, :, 1, :]).reshape(-1).astype(jnp.int32)
    live_mask = (jnp.arange(KMAX, dtype=jnp.int32)[None, None, :] < counts[:, :, None]).astype(jnp.float32).reshape(-1)
    measured_all = patterns.reshape(-1, W, W)
    probe_real = probe[0]
    probe_imag = probe[1]

    def slot_step(carry, inputs):
        gradient, probe_total = carry
        top_row, left_col, alive, measured = inputs
        corner = (jnp.int32(0), top_row, left_col)
        patches = lax.dynamic_slice(padded, corner, (2, W, W))
        object_real = patches[0][None]
        object_imag = patches[1][None]
        wave_real = probe_real * object_real - probe_imag * object_imag
        wave_imag = probe_real * object_imag + probe_imag * object_real
        wavefield = jnp.concatenate([wave_real, wave_imag], axis=-1).astype(jnp.bfloat16)
        far_real, far_imag = transform(wavefield, cosine_table, sine_table, 1.0)
        intensity = lax.optimization_barrier(jnp.sum(far_real * far_real + far_imag * far_imag, axis=0))
        residual = alive * (intensity - measured.astype(jnp.float32))
        weighted = jnp.concatenate([residual[None] * far_real, residual[None] * far_imag], axis=-1).astype(jnp.bfloat16)
        back_real, back_imag = transform(weighted, cosine_table, sine_table, -1.0)
        object_terms = jnp.stack([lax.optimization_barrier(jnp.sum(probe_real * back_real + probe_imag * back_imag, axis=0)), lax.optimization_barrier(jnp.sum(probe_real * back_imag - probe_imag * back_real, axis=0))])
        probe_terms = jnp.stack([object_real * back_real + object_imag * back_imag, object_real * back_imag - object_imag * back_real])
        current = lax.dynamic_slice(gradient, corner, (2, W, W))
        gradient = lax.dynamic_update_slice(gradient, current + object_terms, corner)
        return ((gradient, probe_total + probe_terms), None)
    start = (jnp.zeros(padded.shape, jnp.float32), jnp.zeros(probe.shape, jnp.float32))
    (gradient, probe_total), unused = lax.scan(slot_step, start, (row_start, col_start, live_mask, measured_all))
    object_grad = gradient[:, margin:margin + NY, margin:margin + NX]
    summed_count = jnp.sum(counts.astype(jnp.float32))
    return (object_grad, probe_total / summed_count)
```

```python
import math

import jax
import jax.numpy as jnp
import ml_dtypes
import numpy as np
from jax import lax
from jax.experimental import pallas as pl
from jax.experimental.pallas import tpu as pltpu
from jax.sharding import PartitionSpec as P

W = 256
MODES = 2
KMAX = 8
HALF = W // 2
LANES = 128


def tables():
    counter = np.arange(W)
    phases = (counter[:, None] * counter[None, :] % W).astype(np.float32)
    angles = (np.float32(2.0 * math.pi / W) * phases).astype(np.float32)
    scaling = np.float32(1.0 / math.sqrt(W))
    cosine = (np.cos(angles) * scaling).astype(ml_dtypes.bfloat16)
    sine = (np.sin(angles) * scaling).astype(ml_dtypes.bfloat16)
    ahead = np.block([[cosine, -sine], [sine, cosine]])
    back = np.block([[cosine, sine], [-sine, cosine]])
    return ahead, back


def swap(x, axis, parity):
    size = lax.axis_size(axis)
    pairs = [(i, i + 1) for i in range(parity, size - 1, 2)]
    return lax.ppermute(x, axis, pairs + [(j, i) for i, j in pairs])


def exchange(x, axis, bits):
    size = lax.axis_size(axis)
    return lax.ppermute(x, axis, [(i, i ^ bits) for i in range(size)])


def slots_kernel(
    side_ref,
    offsets_ref,
    count_ref,
    own_ref,
    row_a_ref,
    row_b_ref,
    col_a_ref,
    col_b_ref,
    corner_a_ref,
    corner_b_ref,
    probe_ref,
    patterns_ref,
    ahead_ref,
    back_ref,
    grad_ref,
    probe_grad_ref,
    padded,
    window,
    wave,
    half_ahead,
    far,
    weighted,
    half_back,
    chi,
    sems,
):
    tile = own_ref.shape[1]
    far_edge = tile + HALF
    row_odd = side_ref[0]
    col_odd = side_ref[1]
    row_a = pl.multiple_of((1 - row_odd) * far_edge, LANES)
    row_b = pl.multiple_of(row_odd * far_edge, LANES)
    col_a = pl.multiple_of((1 - col_odd) * far_edge, LANES)
    col_b = pl.multiple_of(col_odd * far_edge, LANES)
    middle = pl.ds(HALF, tile)
    moves = [
        (own_ref, middle, middle),
        (row_a_ref, pl.ds(row_a, HALF), middle),
        (row_b_ref, pl.ds(row_b, HALF), middle),
        (col_a_ref, middle, pl.ds(col_a, HALF)),
        (col_b_ref, middle, pl.ds(col_b, HALF)),
        (corner_a_ref.at[0], pl.ds(row_a, HALF), pl.ds(col_a, HALF)),
        (corner_a_ref.at[1], pl.ds(row_b, HALF), pl.ds(col_a, HALF)),
        (corner_b_ref.at[0], pl.ds(row_a, HALF), pl.ds(col_b, HALF)),
        (corner_b_ref.at[1], pl.ds(row_b, HALF), pl.ds(col_b, HALF)),
    ]
    copies = [
        pltpu.make_async_copy(source, padded.at[:, rows, columns], sems.at[index])
        for index, (source, rows, columns) in enumerate(moves)
    ]
    for copy in copies:
        copy.start()
    grad_ref[...] = jnp.zeros_like(grad_ref)
    probe_grad_ref[...] = jnp.zeros_like(probe_grad_ref)
    for copy in copies:
        copy.wait()
    lane = lax.broadcasted_iota(jnp.int32, (8, LANES), 1)
    sub = lax.broadcasted_iota(jnp.int32, (8, LANES), 0)
    zero = jnp.zeros((8, LANES), jnp.float32)
    step = 32

    def slot(k, carry):
        row = offsets_ref[0, k]
        column = offsets_ref[1, k]
        row_base = pl.multiple_of(row // 8 * 8, 8)
        row_shift = row - row_base
        col_base = pl.multiple_of(column // LANES * LANES, LANES)
        col_shift = column - col_base

        in_lane = lane < LANES - col_shift
        in_sub = sub < 8 - row_shift
        lane_turn = lax.rem(LANES - col_shift, LANES)
        sub_turn = lax.rem(8 - row_shift, 8)

        def lanes_of(plane, group):
            parts = [
                pltpu.roll(
                    padded[
                        plane, pl.ds(row_base + 8 * group, 8), pl.ds(col_base + LANES * j, LANES)
                    ],
                    lane_turn,
                    1,
                )
                for j in range(3)
            ]
            return [
                pltpu.roll(jnp.where(in_lane, parts[j], parts[j + 1]), sub_turn, 0)
                for j in range(2)
            ]

        for plane in range(2):
            before = lanes_of(plane, 0)
            for group in range(W // 8):
                after = lanes_of(plane, group + 1)
                for j in range(2):
                    window[plane, 8 * group : 8 * group + 8, LANES * j : LANES * j + LANES] = (
                        jnp.where(in_sub, before[j], after[j])
                    )
                before = after

        for mode in range(MODES):
            for start in range(0, W, step):
                rows = slice(start, start + step)
                object_real, object_imag = window[0, rows, :], window[1, rows, :]
                probe_real, probe_imag = probe_ref[0, mode, rows, :], probe_ref[1, mode, rows, :]
                into = slice(mode * W + start, mode * W + start + step)
                wave[into, :W] = (probe_real * object_real - probe_imag * object_imag).astype(
                    jnp.bfloat16
                )
                wave[into, W:] = (probe_real * object_imag + probe_imag * object_real).astype(
                    jnp.bfloat16
                )
        halfway = jnp.dot(
            wave[...], ahead_ref[...], preferred_element_type=jnp.float32
        ).astype(jnp.bfloat16)
        for mode in range(MODES):
            rows = slice(mode * W, mode * W + W)
            half_ahead[:W, rows] = halfway[rows, :W]
            half_ahead[W:, rows] = halfway[rows, W:]
        far[...] = jnp.dot(back_ref[...], half_ahead[...], preferred_element_type=jnp.float32)
        for start in range(0, W, step):
            rows = slice(start, start + step)
            imag_rows = slice(W + start, W + start + step)
            reals = [far[rows, m * W : m * W + W] for m in range(MODES)]
            imags = [far[imag_rows, m * W : m * W + W] for m in range(MODES)]
            intensity = sum(r * r + i * i for r, i in zip(reals, imags))
            residual = intensity - patterns_ref[k, rows, :].astype(jnp.float32)
            for m in range(MODES):
                into = slice(m * W + start, m * W + start + step)
                weighted[into, :W] = (residual * reals[m]).astype(jnp.bfloat16)
                weighted[into, W:] = (residual * imags[m]).astype(jnp.bfloat16)
        back_half = jnp.dot(
            weighted[...], back_ref[...], preferred_element_type=jnp.float32
        ).astype(jnp.bfloat16)
        for mode in range(MODES):
            rows = slice(mode * W, mode * W + W)
            half_back[:W, rows] = back_half[rows, :W]
            half_back[W:, rows] = back_half[rows, W:]
        chi[...] = jnp.dot(ahead_ref[...], half_back[...], preferred_element_type=jnp.float32)

        from_lane = lane >= col_shift
        from_sub = sub >= row_shift

        def terms(start, low):
            rows = slice(start, start + 8)
            imag_rows = slice(W + start, W + start + 8)
            columns = slice(low, low + LANES)
            object_real, object_imag = window[0, rows, columns], window[1, rows, columns]
            real, imag = zero, zero
            for m in range(MODES):
                at = slice(m * W + low, m * W + low + LANES)
                chi_real, chi_imag = chi[rows, at], chi[imag_rows, at]
                probe_real = probe_ref[0, m, rows, columns]
                probe_imag = probe_ref[1, m, rows, columns]
                probe_grad_ref[0, m, rows, columns] += (
                    object_real * chi_real + object_imag * chi_imag
                )
                probe_grad_ref[1, m, rows, columns] += (
                    object_real * chi_imag - object_imag * chi_real
                )
                real += probe_real * chi_real + probe_imag * chi_imag
                imag += probe_real * chi_imag - probe_imag * chi_real
            return [
                pltpu.roll(pltpu.roll(value, col_shift, 1), row_shift, 0) for value in (real, imag)
            ]

        before = [[zero, zero], [zero, zero]]
        for group in range(W // 8 + 1):
            if group < W // 8:
                after = [terms(8 * group, 0), terms(8 * group, LANES)]
            else:
                after = [[zero, zero], [zero, zero]]
            rows = pl.ds(row_base + 8 * group, 8)
            for plane in range(2):
                left = jnp.where(from_sub, after[0][plane], before[0][plane])
                right = jnp.where(from_sub, after[1][plane], before[1][plane])
                grad_ref[plane, rows, pl.ds(col_base, LANES)] += jnp.where(from_lane, left, 0.0)
                grad_ref[plane, rows, pl.ds(col_base + LANES, LANES)] += jnp.where(
                    from_lane, right, left
                )
                grad_ref[plane, rows, pl.ds(col_base + 2 * LANES, LANES)] += jnp.where(
                    from_lane, 0.0, right
                )
            before = after
        return carry

    lax.fori_loop(0, count_ref[0], slot, 0)


def slots(sides, offsets, count, own, halos, probe, patterns):
    tile = own.shape[1]
    rows = tile + 2 * HALF + 8
    columns = tile + 2 * HALF + LANES
    smem = pl.BlockSpec(memory_space=pltpu.SMEM)
    vmem = pl.BlockSpec(memory_space=pltpu.VMEM)
    anywhere = pl.BlockSpec(memory_space=pl.ANY)
    ahead, back = tables()
    square = (2 * W, 2 * W)
    return pl.pallas_call(
        slots_kernel,
        out_shape=(
            jax.ShapeDtypeStruct((2, rows, columns), jnp.float32),
            jax.ShapeDtypeStruct((2, MODES, W, W), jnp.float32),
        ),
        in_specs=[smem] * 3 + [anywhere] * 7 + [vmem] * 4,
        out_specs=(vmem, vmem),
        scratch_shapes=[
            pltpu.VMEM((2, rows, columns), jnp.float32),
            pltpu.VMEM((2, W, W), jnp.float32),
            pltpu.VMEM(square, jnp.bfloat16),
            pltpu.VMEM(square, jnp.bfloat16),
            pltpu.VMEM(square, jnp.float32),
            pltpu.VMEM(square, jnp.bfloat16),
            pltpu.VMEM(square, jnp.bfloat16),
            pltpu.VMEM(square, jnp.float32),
            pltpu.SemaphoreType.DMA((9,)),
        ],
        compiler_params=pltpu.CompilerParams(vmem_limit_bytes=50 * 1024 * 1024),
    )(sides, offsets, count, own, *halos, probe, patterns, jnp.asarray(ahead), jnp.asarray(back))


def cut(x, start, size, dim):
    return lax.dynamic_slice_in_dim(x, start, size, axis=dim)


def fold(total, axis):
    size = lax.axis_size(axis)
    me = lax.axis_index(axis)
    bits = 1
    while bits < size:
        mine = (me // bits) % 2
        half = total.shape[0] // 2
        keep = cut(total, mine * half, half, 0)
        away = cut(total, (1 - mine) * half, half, 0)
        total = keep + exchange(away, axis, bits)
        bits *= 2
    return total


def unfold(part, axis):
    size = lax.axis_size(axis)
    me = lax.axis_index(axis)
    bits = size // 2
    while bits:
        mine = (me // bits) % 2
        other = exchange(part, axis, bits)
        part = jnp.where(
            mine == 0, jnp.concatenate([part, other]), jnp.concatenate([other, part])
        )
        bits //= 2
    return part


def summed(value, axes):
    for axis in axes:
        bits = 1
        while bits < lax.axis_size(axis):
            value = value + exchange(value, axis, bits)
            bits *= 2
    return value


def local(object_field, probe, positions, counts, patterns):
    tile = object_field.shape[1]
    edge = tile - HALF
    row_odd = lax.axis_index("row") % 2
    col_odd = lax.axis_index("col") % 2
    live = counts[0, 0]

    row_a = swap(cut(object_field, (1 - row_odd) * edge, HALF, 1), "row", 0)
    row_b = swap(cut(object_field, row_odd * edge, HALF, 1), "row", 1)
    col_a = swap(cut(object_field, (1 - col_odd) * edge, HALF, 2), "col", 0)
    col_b = swap(cut(object_field, col_odd * edge, HALF, 2), "col", 1)
    both = jnp.stack([row_a, row_b])
    corner_a = swap(cut(both, (1 - col_odd) * edge, HALF, 3), "col", 0)
    corner_b = swap(cut(both, col_odd * edge, HALF, 3), "col", 1)
    count = jnp.full((8, LANES), live.astype(jnp.float32))
    total_count = summed(count, ("col", "row"))[0, 0]

    sides = jnp.stack([row_odd, col_odd]).astype(jnp.int32)
    grad, probe_part = slots(
        sides,
        positions[0, 0],
        live[None],
        object_field,
        (row_a, row_b, col_a, col_b, corner_a, corner_b),
        probe,
        patterns[0, 0],
    )

    far_edge = tile + HALF
    top, bottom = grad[:, :HALF], grad[:, far_edge : far_edge + HALF]
    outer = jnp.stack([top, bottom])
    inner = grad[:, HALF:far_edge]
    corner_a = swap(cut(outer, (1 - col_odd) * far_edge, HALF, 3), "col", 0)
    corner_b = swap(cut(outer, col_odd * far_edge, HALF, 3), "col", 1)
    col_a = swap(cut(inner, (1 - col_odd) * far_edge, HALF, 2), "col", 0)
    col_b = swap(cut(inner, col_odd * far_edge, HALF, 2), "col", 1)
    left = jnp.where(col_odd == 1, corner_a, corner_b)
    right = jnp.where(col_odd == 1, corner_b, corner_a)
    outer = outer[..., HALF:far_edge]
    outer = outer.at[..., :HALF].add(left).at[..., edge:].add(right)
    row_a = swap(jnp.where(row_odd == 1, outer[0], outer[1]), "row", 0)
    row_b = swap(jnp.where(row_odd == 1, outer[1], outer[0]), "row", 1)
    result = inner[:, :, HALF:far_edge]
    left = jnp.where(col_odd == 1, col_a, col_b)
    right = jnp.where(col_odd == 1, col_b, col_a)
    result = result.at[:, :, :HALF].add(left).at[:, :, edge:].add(right)
    above = jnp.where(row_odd == 1, row_a, row_b)
    below = jnp.where(row_odd == 1, row_b, row_a)
    result = result.at[:, :HALF].add(above).at[:, edge:].add(below)

    flat = probe_part.reshape(-1, W)
    part = fold(fold(flat, "col"), "row")
    whole = unfold(unfold(part, "row"), "col")
    return result, whole.reshape(probe.shape) / total_count


def solution(mesh):
    placed = (
        P(None, ("groups", "row"), "col"),
        P(None, "groups", None, None),
        P(("groups", "row"), "col", None, None),
        P(("groups", "row"), "col"),
        P(("groups", "row"), "col", None, None, None),
    )
    return jax.shard_map(
        local,
        mesh=mesh,
        in_specs=placed,
        out_specs=(P(None, ("groups", "row"), "col"), P(None, "groups", None, None)),
        check_vma=False,
    )
```

```python
import functools
import math

import jax
import jax.numpy as jnp
import ml_dtypes
import numpy as np
from jax import lax
from jax.experimental import pallas as pl
from jax.experimental.pallas import tpu as pltpu
from jax.sharding import PartitionSpec as P

W = 256
MODES = 2
KMAX = 8
HALF = W // 2
LANES = 128
GROUPS = W // 8
VMEM_BYTES = 50 * 1024 * 1024


def tables():
    counter = np.arange(W)
    phases = (counter[:, None] * counter[None, :] % W).astype(np.float32)
    angles = (np.float32(2.0 * math.pi / W) * phases).astype(np.float32)
    scaling = np.float32(1.0 / math.sqrt(W))
    cosine = (np.cos(angles) * scaling).astype(ml_dtypes.bfloat16)
    sine = (np.sin(angles) * scaling).astype(ml_dtypes.bfloat16)
    ahead = np.block([[cosine, -sine], [sine, cosine]])
    back = np.block([[cosine, sine], [-sine, cosine]])
    return ahead, back


def side_pairs(size, parity):
    pairs = [(i, i + 1) for i in range(parity, size - 1, 2)]
    return pairs + [(j, i) for i, j in pairs]


def swap(x, axis, parity):
    return lax.ppermute(x, axis, side_pairs(lax.axis_size(axis), parity))


def exchange(x, axis, bits):
    size = lax.axis_size(axis)
    return lax.ppermute(x, axis, [(i, i ^ bits) for i in range(size)])


def edges(side_ref, tile):
    far_edge = tile + HALF
    row_odd, col_odd = side_ref[0], side_ref[1]
    row_a = pl.multiple_of((1 - row_odd) * far_edge, LANES)
    row_b = pl.multiple_of(row_odd * far_edge, LANES)
    col_a = pl.multiple_of((1 - col_odd) * far_edge, LANES)
    col_b = pl.multiple_of(col_odd * far_edge, LANES)
    return [pl.ds(start, HALF) for start in (row_a, row_b, col_a, col_b)]


def inner_edges(side_ref, tile):
    edge = tile - HALF
    row_odd, col_odd = side_ref[0], side_ref[1]
    row_a = pl.multiple_of((1 - row_odd) * edge, LANES)
    row_b = pl.multiple_of(row_odd * edge, LANES)
    col_a = pl.multiple_of((1 - col_odd) * edge, LANES)
    col_b = pl.multiple_of(col_odd * edge, LANES)
    return [pl.ds(start, HALF) for start in (row_a, row_b, col_a, col_b)]


def run_copies(moves, sems):
    copies = [
        pltpu.make_async_copy(source, target, sems.at[index])
        for index, (source, target) in enumerate(moves)
    ]
    for copy in copies:
        copy.start()
    return copies


def merge(first, second):
    order = [((i + 0.5) / len(first), 0, step) for i, step in enumerate(first)]
    order += [((i + 0.5) / len(second), 1, step) for i, step in enumerate(second)]
    for _, _, step in sorted(order, key=lambda entry: entry[:2]):
        step()


def slots_kernel(
    pieces,
    side_ref,
    offsets_ref,
    count_ref,
    own_ref,
    row_a_ref,
    row_b_ref,
    col_a_ref,
    col_b_ref,
    corner_a_ref,
    corner_b_ref,
    probe_in,
    patterns_in,
    ahead_in,
    back_in,
    probe_keep,
    probe_away,
    inner_out,
    row_a_out,
    row_b_out,
    col_a_out,
    col_b_out,
    corner_out,
    padded,
    grad,
    probe_grad,
    windows,
    *rest,
):
    sets = (rest[0:6], rest[6:12])
    probe_ref, patterns_ref, ahead_ref, back_ref, counted, sems = rest[12:]
    tile = own_ref.shape[1]
    row_a, row_b, col_a, col_b = edges(side_ref, tile)
    middle = pl.ds(HALF, tile)
    copies = run_copies(
        [
            (own_ref, padded.at[:, middle, middle]),
            (row_a_ref, padded.at[:, row_a, middle]),
            (row_b_ref, padded.at[:, row_b, middle]),
            (col_a_ref, padded.at[:, middle, col_a]),
            (col_b_ref, padded.at[:, middle, col_b]),
            (corner_a_ref.at[0], padded.at[:, row_a, col_a]),
            (corner_a_ref.at[1], padded.at[:, row_b, col_a]),
            (corner_b_ref.at[0], padded.at[:, row_a, col_b]),
            (corner_b_ref.at[1], padded.at[:, row_b, col_b]),
            (probe_in, probe_ref),
            (patterns_in, patterns_ref),
            (ahead_in, ahead_ref),
            (back_in, back_ref),
        ],
        sems,
    )
    grad[...] = jnp.zeros_like(grad)
    probe_grad[...] = jnp.zeros_like(probe_grad)
    for buffers in sets:
        buffers[5][...] = jnp.zeros_like(buffers[5])
    for index in (2, 3):
        windows[index] = jnp.zeros(windows.shape[1:], jnp.float32)
    for copy in copies:
        copy.wait()
    lane = lax.broadcasted_iota(jnp.int32, (8, LANES), 1)
    sub = lax.broadcasted_iota(jnp.int32, (8, LANES), 0)
    zero = jnp.zeros((8, LANES), jnp.float32)
    batch = 4
    step = 8 * batch

    def place(k):
        row, column = offsets_ref[0, k], offsets_ref[1, k]
        row_base = pl.multiple_of(row // 8 * 8, 8)
        col_base = pl.multiple_of(column // LANES * LANES, LANES)
        return row_base, row - row_base, col_base, column - col_base

    def make_wave(k, buffers, w):
        wave = buffers[0]
        row_base, row_shift, col_base, col_shift = place(k)
        in_lane, in_sub = lane < LANES - col_shift, sub < 8 - row_shift
        lane_turn = lax.rem(LANES - col_shift, LANES)
        sub_turn = lax.rem(8 - row_shift, 8)
        before = {}

        def turned(plane, group):
            rows = pl.ds(row_base + 8 * group, 8)
            parts = [
                pltpu.roll(padded[plane, rows, pl.ds(col_base + LANES * j, LANES)], lane_turn, 1)
                for j in range(3)
            ]
            return [
                pltpu.roll(jnp.where(in_lane, parts[j], parts[j + 1]), sub_turn, 0)
                for j in range(2)
            ]

        def some_rows(first):
            if first == 0:
                for plane in range(2):
                    before[plane] = turned(plane, 0)
            pieces = [[], []]
            for group in range(first, first + batch):
                for plane in range(2):
                    after = turned(plane, group + 1)
                    value = jnp.concatenate(
                        [jnp.where(in_sub, b, a) for b, a in zip(before[plane], after)], axis=1
                    )
                    windows[w, plane, 8 * group : 8 * group + 8, :] = value
                    pieces[plane].append(value)
                    before[plane] = after
            object_real, object_imag = [jnp.concatenate(piece, axis=0) for piece in pieces]
            start = 8 * first
            rows = slice(start, start + step)
            for m in range(MODES):
                probe_real, probe_imag = probe_ref[0, m, rows, :], probe_ref[1, m, rows, :]
                into = slice(m * W + start, m * W + start + step)
                wave[into, :W] = (probe_real * object_real - probe_imag * object_imag).astype(
                    jnp.bfloat16
                )
                wave[into, W:] = (probe_real * object_imag + probe_imag * object_real).astype(
                    jnp.bfloat16
                )

        return [functools.partial(some_rows, first) for first in range(0, GROUPS, batch)]

    def right(source, table, target, m):
        rows = slice(m * W, m * W + W)
        product = jnp.dot(
            source[rows, :], table[...], preferred_element_type=jnp.float32
        ).astype(jnp.bfloat16)
        target[:W, rows] = product[:, :W]
        target[W:, rows] = product[:, W:]

    def left(source, table, target, m):
        columns = slice(m * W, m * W + W)
        target[:, columns] = jnp.dot(
            table[...], source[:, columns], preferred_element_type=jnp.float32
        )

    def ahead_right(buffers, m):
        return functools.partial(right, buffers[0], ahead_ref, buffers[1], m)

    def ahead_left(buffers, m):
        return functools.partial(left, buffers[1], back_ref, buffers[2], m)

    def back_right(buffers, m):
        return functools.partial(right, buffers[3], back_ref, buffers[4], m)

    def back_left(buffers, m):
        return functools.partial(left, buffers[4], ahead_ref, buffers[5], m)

    def weigh(k, live, buffers):
        far, weighted = buffers[2], buffers[3]

        def some_rows(start):
            rows = slice(start, start + step)
            imag_rows = slice(W + start, W + start + step)
            reals = [far[rows, m * W : m * W + W] for m in range(MODES)]
            imags = [far[imag_rows, m * W : m * W + W] for m in range(MODES)]
            intensity = sum(r * r + i * i for r, i in zip(reals, imags))
            residual = intensity - patterns_ref[k, rows, :].astype(jnp.float32)
            if live is not None:
                residual = residual * live
            for m in range(MODES):
                into = slice(m * W + start, m * W + start + step)
                weighted[into, :W] = (residual * reals[m]).astype(jnp.bfloat16)
                weighted[into, W:] = (residual * imags[m]).astype(jnp.bfloat16)

        return [functools.partial(some_rows, start) for start in range(0, W, step)]

    def add_terms(members):
        info = []
        for k, _, _ in members:
            row_base, row_shift, col_base, col_shift = place(k)
            info.append(
                (row_base, row_shift, col_base, col_shift, lane >= col_shift, sub >= row_shift)
            )

        def terms(start, low):
            rows = slice(start, start + 8)
            imag_rows = slice(W + start, W + start + 8)
            columns = slice(low, low + LANES)
            turned = []
            totals = [[None, None] for _ in range(MODES)]
            probes = [[probe_ref[plane, m, rows, columns] for plane in range(2)] for m in range(MODES)]
            for (_, buffers, w), (_, row_shift, _, col_shift, _, _) in zip(members, info):
                chi = buffers[5]
                object_real, object_imag = windows[w, 0, rows, columns], windows[w, 1, rows, columns]
                sums = [None, None]
                for m in range(MODES):
                    at = slice(m * W + low, m * W + low + LANES)
                    chi_real, chi_imag = chi[rows, at], chi[imag_rows, at]
                    probe_real, probe_imag = probes[m]
                    mine = (
                        object_real * chi_real + object_imag * chi_imag,
                        object_real * chi_imag - object_imag * chi_real,
                    )
                    more = (
                        probe_real * chi_real + probe_imag * chi_imag,
                        probe_real * chi_imag - probe_imag * chi_real,
                    )
                    for plane in range(2):
                        total = totals[m][plane]
                        totals[m][plane] = mine[plane] if total is None else total + mine[plane]
                        total = sums[plane]
                        sums[plane] = more[plane] if total is None else total + more[plane]
                turned.append(
                    [pltpu.roll(pltpu.roll(value, col_shift, 1), row_shift, 0) for value in sums]
                )
            for m in range(MODES):
                for plane in range(2):
                    probe_grad[plane, m, rows, columns] += totals[m][plane]
            return turned

        nothing = [[zero, zero] for _ in members]
        before = [nothing, nothing]

        def some_groups(first):
            groups = range(first, min(first + batch, GROUPS + 1))
            news = []
            for group in groups:
                if group < GROUPS:
                    news.append([terms(8 * group, 0), terms(8 * group, LANES)])
                else:
                    news.append([nothing, nothing])
            for q, (row_base, _, col_base, _, from_lane, from_sub) in enumerate(info):
                adds = []
                last = [before[0][q], before[1][q]]
                for group, new in zip(groups, news):
                    rows = pl.ds(row_base + 8 * group, 8)
                    for plane in range(2):
                        low, high = [
                            jnp.where(from_sub, new[half][q][plane], last[half][plane])
                            for half in range(2)
                        ]
                        values = (
                            jnp.where(from_lane, low, 0.0),
                            jnp.where(from_lane, high, low),
                            jnp.where(from_lane, 0.0, high),
                        )
                        for j, value in enumerate(values):
                            adds.append((plane, rows, pl.ds(col_base + LANES * j, LANES), value))
                    last = [new[0][q], new[1][q]]
                olds = [grad[plane, rows, columns] for plane, rows, columns, _ in adds]
                for (plane, rows, columns, value), old in zip(adds, olds):
                    grad[plane, rows, columns] = old + value
            before[:] = news[-1]

        return [functools.partial(some_groups, first) for first in range(0, GROUPS + 1, batch)]

    count = count_ref[0]
    pairs = (count + 1) // 2
    x, y = sets
    for each in make_wave(0, x, 0) + make_wave(1, y, 1):
        each()

    def pair(index, carry):
        now = (2 * index, 2 * index + 1)
        past = [jnp.maximum(k - 2, 0) for k in now]
        later = [jnp.minimum(k + 2, KMAX - 1) for k in now]
        other = 2 - lax.rem(index, 2) * 2
        live = (now[1] < count).astype(jnp.float32)
        adds = add_terms([(past[0], x, other), (past[1], y, other + 1)])
        some = len(adds) * 2 // 3
        merge(
            [ahead_right(b, m) for b in sets for m in range(MODES)]
            + [ahead_left(x, m) for m in range(MODES)],
            adds[:some],
        )
        merge([ahead_left(y, m) for m in range(MODES)], adds[some:] + weigh(now[0], None, x))
        merge([back_right(x, m) for m in range(MODES)], weigh(now[1], live, y))
        merge(
            [back_right(y, m) for m in range(MODES)]
            + [back_left(b, m) for b in sets for m in range(MODES)],
            make_wave(later[0], x, other) + make_wave(later[1], y, other + 1),
        )
        return carry

    lax.fori_loop(0, pairs, pair, 0)
    final = pairs - 1
    at = lax.rem(final, 2) * 2
    for each in add_terms([(2 * final, x, at), (2 * final + 1, y, at + 1)]):
        each()

    moves = [
        (grad.at[:, middle, middle], inner_out),
        (grad.at[:, row_a, middle], row_a_out.at[:, :, pl.ds(0, tile)]),
        (grad.at[:, row_b, middle], row_b_out.at[:, :, pl.ds(0, tile)]),
        (grad.at[:, row_a, col_b], row_a_out.at[:, :, pl.ds(tile, HALF)]),
        (grad.at[:, row_b, col_b], row_b_out.at[:, :, pl.ds(tile, HALF)]),
        (grad.at[:, middle, col_a], col_a_out),
        (grad.at[:, middle, col_b], col_b_out),
        (grad.at[:, row_a, col_a], corner_out.at[0]),
        (grad.at[:, row_b, col_a], corner_out.at[1]),
    ]
    me = side_ref[2]
    half_rows = probe_keep.shape[0] - 8
    height = 2 * half_rows // pieces
    per_square = W // height
    for piece in range(pieces):
        which = piece ^ me
        square, block = which // per_square, lax.rem(which, per_square)
        source = probe_grad.at[
            square // MODES, lax.rem(square, MODES), pl.ds(pl.multiple_of(block * height, 8), height)
        ]
        target = probe_keep if piece < pieces // 2 else probe_away
        moves.append((source, target.at[pl.ds(piece % (pieces // 2) * height, height)]))
    counted[...] = jnp.full(counted.shape, count.astype(jnp.float32))
    moves += [(counted, target.at[pl.ds(half_rows, 8)]) for target in (probe_keep, probe_away)]
    for copy in run_copies(moves, sems):
        copy.wait()


def slots(sides, offsets, count, own, halos, probe, patterns, pieces):
    tile = own.shape[1]
    wide = tile + 2 * HALF
    smem = pl.BlockSpec(memory_space=pltpu.SMEM)
    anywhere = pl.BlockSpec(memory_space=pl.ANY)
    ahead, back = tables()
    square = (2 * W, 2 * W)
    buffers = [
        pltpu.VMEM(square, kind)
        for kind in (jnp.bfloat16, jnp.bfloat16, jnp.float32, jnp.bfloat16, jnp.bfloat16, jnp.float32)
    ]
    outs = [
        (MODES * W + 8, W),
        (MODES * W + 8, W),
        (2, tile, tile),
        (2, HALF, tile + HALF),
        (2, HALF, tile + HALF),
        (2, tile, HALF),
        (2, tile, HALF),
        (2, 2, HALF, HALF),
    ]
    return pl.pallas_call(
        functools.partial(slots_kernel, pieces),
        out_shape=[jax.ShapeDtypeStruct(shape, jnp.float32) for shape in outs],
        in_specs=[smem] * 3 + [pl.BlockSpec(memory_space=pltpu.HBM)] * 11,
        out_specs=[anywhere] * len(outs),
        scratch_shapes=[
            pltpu.VMEM((2, wide, wide), jnp.float32),
            pltpu.VMEM((2, wide, wide), jnp.float32),
            pltpu.VMEM((2, MODES, W, W), jnp.float32),
            pltpu.VMEM((4, 2, W, W), jnp.float32),
            *buffers,
            *buffers,
            pltpu.VMEM(probe.shape, jnp.float32),
            pltpu.VMEM(patterns.shape, patterns.dtype),
            pltpu.VMEM(square, jnp.bfloat16),
            pltpu.VMEM(square, jnp.bfloat16),
            pltpu.VMEM((8, W), jnp.float32),
            pltpu.SemaphoreType.DMA((13 + pieces,)),
        ],
        compiler_params=pltpu.CompilerParams(vmem_limit_bytes=VMEM_BYTES),
    )(sides, offsets, count, own, *halos, probe, patterns, jnp.asarray(ahead), jnp.asarray(back))


def join_kernel(
    side_ref, inner_ref, row_a_ref, row_b_ref, col_a_ref, col_b_ref, out_ref
):
    row_a, row_b, col_a, col_b = inner_edges(side_ref, inner_ref.shape[1])
    out_ref[...] = inner_ref[...]
    out_ref[:, row_a, :] += row_a_ref[...]
    out_ref[:, row_b, :] += row_b_ref[...]
    out_ref[:, :, col_a] += col_a_ref[...]
    out_ref[:, :, col_b] += col_b_ref[...]


def join(sides, inner, *terms):
    vmem = pl.BlockSpec(memory_space=pltpu.VMEM)
    return pl.pallas_call(
        join_kernel,
        out_shape=jax.ShapeDtypeStruct(inner.shape, jnp.float32),
        in_specs=[pl.BlockSpec(memory_space=pltpu.SMEM)] + [vmem] * (1 + len(terms)),
        out_specs=vmem,
        compiler_params=pltpu.CompilerParams(vmem_limit_bytes=VMEM_BYTES),
    )(sides, inner, *terms)


def cut(x, start, dim):
    return lax.dynamic_slice_in_dim(x, start, HALF, axis=dim)


def add_at(strip, term, start):
    old = lax.dynamic_slice_in_dim(strip, start, term.shape[2], axis=2)
    return lax.dynamic_update_slice_in_dim(strip, old + term, start, axis=2)


def gathered(part, axis, bits):
    other = exchange(part, axis, bits)
    first = lax.axis_index(axis) // bits % 2 == 0
    return jnp.where(first, jnp.concatenate([part, other]), jnp.concatenate([other, part]))


def local(object_field, probe, positions, counts, patterns):
    tile = object_field.shape[1]
    edge = tile - HALF
    barrier = lax.optimization_barrier
    row, col = lax.axis_index("row"), lax.axis_index("col")
    live = counts[0, 0]
    halvings = [
        (axis, 1 << i)
        for axis in ("col", "row")
        for i in range(lax.axis_size(axis).bit_length() - 1)
    ]
    halvings, last = halvings[:-1], halvings[-1]
    pieces = 1 << len(halvings)
    mine = 0
    for axis, bits in halvings:
        mine = 2 * mine + lax.axis_index(axis) // bits % 2
    sides = jnp.stack([row % 2, col % 2, mine]).astype(jnp.int32)

    row_a = swap(cut(object_field, (1 - row % 2) * edge, 1), "row", 0)
    row_b = swap(cut(object_field, row % 2 * edge, 1), "row", 1)
    col_a = swap(cut(object_field, (1 - col % 2) * edge, 2), "col", 0)
    col_b = swap(cut(object_field, col % 2 * edge, 2), "col", 1)
    corner_a = jnp.stack([cut(strip, (1 - col % 2) * edge, 2) for strip in (row_a, row_b)])
    corner_b = jnp.stack([cut(strip, col % 2 * edge, 2) for strip in (row_a, row_b)])
    corner_b = swap(corner_b, "col", 1)
    corner_a = swap(corner_a, "col", 0)

    keep, away, inner, row_a, row_b, col_a, col_b, corner = slots(
        sides,
        positions[0, 0],
        live[None],
        object_field,
        (row_a, row_b, col_a, col_b, corner_a, corner_b),
        probe,
        patterns[0, 0],
        pieces,
    )

    corner = swap(corner, "col", 0)
    away = exchange(away, *halvings[0])
    row_a = swap(add_at(row_a, corner[0], (1 - col % 2) * edge), "row", 0)
    row_b = swap(add_at(row_b, corner[1], (1 - col % 2) * edge), "row", 1)
    keep = keep + away
    col_a = swap(col_a, "col", 0)
    for index, (axis, bits) in enumerate(halvings[1:]):
        half = (keep.shape[0] - 8) // 2
        keep = jnp.concatenate([keep[:half], keep[-8:]]) + exchange(keep[half:], axis, bits)
        if index == 0:
            keep, row_a, row_b, col_a, col_b = barrier((keep, row_a, row_b, col_a, col_b))
            top, bottom = [
                jnp.where(row % 2 == 1, first, second)[:, :, tile:]
                for first, second in ((row_a, row_b), (row_b, row_a))
            ]
            blank = jnp.zeros((2, tile - 2 * HALF, HALF), jnp.float32)
            col_b = swap(col_b + jnp.concatenate([top, blank, bottom], axis=1), "col", 1)
    keep = keep + exchange(keep, *last)
    part = keep[:-8] / keep[-8:-7]
    for axis, bits in reversed(halvings):
        if bits == 1 and axis == "row":
            part = gathered(part, axis, bits)
            part, col_b = barrier((part, col_b))
        elif (axis, bits) != halvings[0]:
            part = gathered(part, axis, bits)
    result = join(sides, inner, row_a[:, :, :tile], row_b[:, :, :tile], col_a, col_b)
    part, result = barrier((part, result))
    whole = gathered(part, *halvings[0])
    return result, whole.reshape(probe.shape)


def solution(mesh):
    placed = (
        P(None, ("groups", "row"), "col"),
        P(None, "groups", None, None),
        P(("groups", "row"), "col", None, None),
        P(("groups", "row"), "col"),
        P(("groups", "row"), "col", None, None, None),
    )
    return jax.shard_map(
        local,
        mesh=mesh,
        in_specs=placed,
        out_specs=(P(None, ("groups", "row"), "col"), P(None, "groups", None, None)),
        check_vma=False,
    )
```

```python
import functools
import math

import jax
import jax.numpy as jnp
import ml_dtypes
import numpy as np
from jax import lax
from jax.experimental import pallas as pl
from jax.experimental.pallas import tpu as pltpu
from jax.sharding import PartitionSpec as P

W = 256
MODES = 2
KMAX = 8
HALF = W // 2
LANES = 128
GROUPS = W // 8
VMEM_BYTES = 50 * 1024 * 1024


def tables():
    counter = np.arange(W)
    phases = (counter[:, None] * counter[None, :] % W).astype(np.float32)
    angles = (np.float32(2.0 * math.pi / W) * phases).astype(np.float32)
    scaling = np.float32(1.0 / math.sqrt(W))
    cosine = (np.cos(angles) * scaling).astype(ml_dtypes.bfloat16)
    sine = (np.sin(angles) * scaling).astype(ml_dtypes.bfloat16)
    ahead = np.block([[cosine, -sine], [sine, cosine]])
    back = np.block([[cosine, sine], [-sine, cosine]])
    return ahead, back


def side_pairs(size, parity):
    pairs = [(i, i + 1) for i in range(parity, size - 1, 2)]
    return pairs + [(j, i) for i, j in pairs]


def swap(x, axis, parity):
    return lax.ppermute(x, axis, side_pairs(lax.axis_size(axis), parity))


def exchange(x, axis, bits):
    size = lax.axis_size(axis)
    return lax.ppermute(x, axis, [(i, i ^ bits) for i in range(size)])


def edges(side_ref, tile):
    far_edge = tile + HALF
    row_odd, col_odd = side_ref[0], side_ref[1]
    row_a = pl.multiple_of((1 - row_odd) * far_edge, LANES)
    row_b = pl.multiple_of(row_odd * far_edge, LANES)
    col_a = pl.multiple_of((1 - col_odd) * far_edge, LANES)
    col_b = pl.multiple_of(col_odd * far_edge, LANES)
    return [pl.ds(start, HALF) for start in (row_a, row_b, col_a, col_b)]


def inner_edges(side_ref, tile):
    edge = tile - HALF
    row_odd, col_odd = side_ref[0], side_ref[1]
    row_a = pl.multiple_of((1 - row_odd) * edge, LANES)
    row_b = pl.multiple_of(row_odd * edge, LANES)
    col_a = pl.multiple_of((1 - col_odd) * edge, LANES)
    col_b = pl.multiple_of(col_odd * edge, LANES)
    return [pl.ds(start, HALF) for start in (row_a, row_b, col_a, col_b)]


def run_copies(moves, sems):
    copies = [
        pltpu.make_async_copy(source, target, sems.at[index])
        for index, (source, target) in enumerate(moves)
    ]
    for copy in copies:
        copy.start()
    return copies


def merge(first, second):
    order = [((i + 0.5) / len(first), 0, step) for i, step in enumerate(first)]
    order += [((i + 0.5) / len(second), 1, step) for i, step in enumerate(second)]
    for _, _, step in sorted(order, key=lambda entry: entry[:2]):
        step()


def slots_kernel(
    pieces,
    side_ref,
    offsets_ref,
    count_ref,
    own_ref,
    row_a_ref,
    row_b_ref,
    col_a_ref,
    col_b_ref,
    corner_a_ref,
    corner_b_ref,
    probe_in,
    patterns_in,
    ahead_in,
    back_in,
    probe_keep,
    probe_away,
    inner_out,
    row_a_out,
    row_b_out,
    col_a_out,
    col_b_out,
    corner_out,
    padded,
    grad,
    probe_grad,
    windows,
    *rest,
):
    sets = (rest[0:6], rest[6:12])
    probe_ref, patterns_ref, ahead_ref, back_ref, counted, sems = rest[12:]
    tile = own_ref.shape[1]
    row_a, row_b, col_a, col_b = edges(side_ref, tile)
    middle = pl.ds(HALF, tile)
    copies = run_copies(
        [
            (own_ref, padded.at[:, middle, middle]),
            (row_a_ref, padded.at[:, row_a, middle]),
            (row_b_ref, padded.at[:, row_b, middle]),
            (col_a_ref, padded.at[:, middle, col_a]),
            (col_b_ref, padded.at[:, middle, col_b]),
            (corner_a_ref.at[0], padded.at[:, row_a, col_a]),
            (corner_a_ref.at[1], padded.at[:, row_b, col_a]),
            (corner_b_ref.at[0], padded.at[:, row_a, col_b]),
            (corner_b_ref.at[1], padded.at[:, row_b, col_b]),
            (probe_in, probe_ref),
            (patterns_in, patterns_ref),
            (ahead_in, ahead_ref),
            (back_in, back_ref),
        ],
        sems,
    )
    grad[...] = jnp.zeros_like(grad)
    probe_grad[...] = jnp.zeros_like(probe_grad)
    for buffers in sets:
        buffers[5][...] = jnp.zeros_like(buffers[5])
    for index in (2, 3):
        windows[index] = jnp.zeros(windows.shape[1:], jnp.float32)
    for copy in copies[:-3]:
        copy.wait()
    lane = lax.broadcasted_iota(jnp.int32, (8, LANES), 1)
    sub = lax.broadcasted_iota(jnp.int32, (8, LANES), 0)
    zero = jnp.zeros((8, LANES), jnp.float32)
    batch = 4
    step = 8 * batch

    def place(k):
        row, column = offsets_ref[0, k], offsets_ref[1, k]
        row_base = pl.multiple_of(row // 8 * 8, 8)
        col_base = pl.multiple_of(column // LANES * LANES, LANES)
        return row_base, row - row_base, col_base, column - col_base

    def make_wave(k, buffers, w):
        wave = buffers[0]
        row_base, row_shift, col_base, col_shift = place(k)
        in_lane, in_sub = lane < LANES - col_shift, sub < 8 - row_shift
        lane_turn = lax.rem(LANES - col_shift, LANES)
        sub_turn = lax.rem(8 - row_shift, 8)
        before = {}

        def turned(plane, group):
            rows = pl.ds(row_base + 8 * group, 8)
            parts = [
                pltpu.roll(padded[plane, rows, pl.ds(col_base + LANES * j, LANES)], lane_turn, 1)
                for j in range(3)
            ]
            return [
                pltpu.roll(jnp.where(in_lane, parts[j], parts[j + 1]), sub_turn, 0)
                for j in range(2)
            ]

        def some_rows(first):
            if first == 0:
                for plane in range(2):
                    before[plane] = turned(plane, 0)
            pieces = [[], []]
            for group in range(first, first + batch):
                for plane in range(2):
                    after = turned(plane, group + 1)
                    value = jnp.concatenate(
                        [jnp.where(in_sub, b, a) for b, a in zip(before[plane], after)], axis=1
                    )
                    windows[w, plane, 8 * group : 8 * group + 8, :] = value
                    pieces[plane].append(value)
                    before[plane] = after
            object_real, object_imag = [jnp.concatenate(piece, axis=0) for piece in pieces]
            start = 8 * first
            rows = slice(start, start + step)
            for m in range(MODES):
                probe_real, probe_imag = probe_ref[0, m, rows, :], probe_ref[1, m, rows, :]
                into = slice(m * W + start, m * W + start + step)
                wave[into, :W] = (probe_real * object_real - probe_imag * object_imag).astype(
                    jnp.bfloat16
                )
                wave[into, W:] = (probe_real * object_imag + probe_imag * object_real).astype(
                    jnp.bfloat16
                )

        return [functools.partial(some_rows, first) for first in range(0, GROUPS, batch)]

    def right(source, table, target):
        product = jnp.dot(
            source[...], table[...], preferred_element_type=jnp.float32
        ).astype(jnp.bfloat16)
        for m in range(MODES):
            rows = slice(m * W, m * W + W)
            target[:W, rows] = product[rows, :W]
            target[W:, rows] = product[rows, W:]

    def left(source, table, target, m):
        columns = slice(m * W, m * W + W)
        target[:, columns] = jnp.dot(
            table[...], source[:, columns], preferred_element_type=jnp.float32
        )

    def ahead_right(buffers):
        return functools.partial(right, buffers[0], ahead_ref, buffers[1])

    def ahead_left(buffers, m):
        return functools.partial(left, buffers[1], back_ref, buffers[2], m)

    def back_right(buffers):
        return functools.partial(right, buffers[3], back_ref, buffers[4])

    def back_left(buffers, m):
        return functools.partial(left, buffers[4], ahead_ref, buffers[5], m)

    def weigh(k, live, buffers):
        far, weighted = buffers[2], buffers[3]

        def some_rows(start):
            rows = slice(start, start + step)
            imag_rows = slice(W + start, W + start + step)
            reals = [far[rows, m * W : m * W + W] for m in range(MODES)]
            imags = [far[imag_rows, m * W : m * W + W] for m in range(MODES)]
            intensity = sum(r * r + i * i for r, i in zip(reals, imags))
            residual = intensity - patterns_ref[k, rows, :].astype(jnp.float32)
            if live is not None:
                residual = residual * live
            for m in range(MODES):
                into = slice(m * W + start, m * W + start + step)
                weighted[into, :W] = (residual * reals[m]).astype(jnp.bfloat16)
                weighted[into, W:] = (residual * imags[m]).astype(jnp.bfloat16)

        return [functools.partial(some_rows, start) for start in range(0, W, step)]

    def add_terms(members):
        info = []
        for k, _, _ in members:
            row_base, row_shift, col_base, col_shift = place(k)
            info.append(
                (row_base, row_shift, col_base, col_shift, lane >= col_shift, sub >= row_shift)
            )

        def terms(start, low):
            rows = slice(start, start + 8)
            imag_rows = slice(W + start, W + start + 8)
            columns = slice(low, low + LANES)
            turned = []
            totals = [[None, None] for _ in range(MODES)]
            probes = [[probe_ref[plane, m, rows, columns] for plane in range(2)] for m in range(MODES)]
            for (_, buffers, w), (_, row_shift, _, col_shift, _, _) in zip(members, info):
                chi = buffers[5]
                object_real, object_imag = windows[w, 0, rows, columns], windows[w, 1, rows, columns]
                sums = [None, None]
                for m in range(MODES):
                    at = slice(m * W + low, m * W + low + LANES)
                    chi_real, chi_imag = chi[rows, at], chi[imag_rows, at]
                    probe_real, probe_imag = probes[m]
                    mine = (
                        object_real * chi_real + object_imag * chi_imag,
                        object_real * chi_imag - object_imag * chi_real,
                    )
                    more = (
                        probe_real * chi_real + probe_imag * chi_imag,
                        probe_real * chi_imag - probe_imag * chi_real,
                    )
                    for plane in range(2):
                        total = totals[m][plane]
                        totals[m][plane] = mine[plane] if total is None else total + mine[plane]
                        total = sums[plane]
                        sums[plane] = more[plane] if total is None else total + more[plane]
                turned.append(
                    [pltpu.roll(pltpu.roll(value, col_shift, 1), row_shift, 0) for value in sums]
                )
            for m in range(MODES):
                for plane in range(2):
                    probe_grad[plane, m, rows, columns] += totals[m][plane]
            return turned

        nothing = [[zero, zero] for _ in members]
        before = [nothing, nothing]

        def some_groups(first):
            groups = range(first, min(first + batch, GROUPS + 1))
            news = []
            for group in groups:
                if group < GROUPS:
                    news.append([terms(8 * group, 0), terms(8 * group, LANES)])
                else:
                    news.append([nothing, nothing])
            for q, (row_base, _, col_base, _, from_lane, from_sub) in enumerate(info):
                adds = []
                last = [before[0][q], before[1][q]]
                for group, new in zip(groups, news):
                    rows = pl.ds(row_base + 8 * group, 8)
                    for plane in range(2):
                        low, high = [
                            jnp.where(from_sub, new[half][q][plane], last[half][plane])
                            for half in range(2)
                        ]
                        values = (
                            jnp.where(from_lane, low, 0.0),
                            jnp.where(from_lane, high, low),
                            jnp.where(from_lane, 0.0, high),
                        )
                        for j, value in enumerate(values):
                            adds.append((plane, rows, pl.ds(col_base + LANES * j, LANES), value))
                    last = [new[0][q], new[1][q]]
                olds = [grad[plane, rows, columns] for plane, rows, columns, _ in adds]
                for (plane, rows, columns, value), old in zip(adds, olds):
                    grad[plane, rows, columns] = old + value
            before[:] = news[-1]

        return [functools.partial(some_groups, first) for first in range(0, GROUPS + 1, batch)]

    count = count_ref[0]
    pairs = (count + 1) // 2
    x, y = sets
    for each in make_wave(0, x, 0) + make_wave(1, y, 1):
        each()
    for copy in copies[-3:]:
        copy.wait()

    def pair(index, carry):
        now = (2 * index, 2 * index + 1)
        past = [jnp.maximum(k - 2, 0) for k in now]
        later = [jnp.minimum(k + 2, KMAX - 1) for k in now]
        other = 2 - lax.rem(index, 2) * 2
        live = (now[1] < count).astype(jnp.float32)
        adds = add_terms([(past[0], x, other), (past[1], y, other + 1)])
        some = len(adds) * 2 // 3
        merge(
            [ahead_right(b) for b in sets]
            + [ahead_left(x, m) for m in range(MODES)],
            adds[:some],
        )
        merge([ahead_left(y, m) for m in range(MODES)], adds[some:] + weigh(now[0], None, x))
        merge([back_right(x)], weigh(now[1], live, y))
        merge(
            [back_right(y)]
            + [back_left(b, m) for b in sets for m in range(MODES)],
            make_wave(later[0], x, other) + make_wave(later[1], y, other + 1),
        )
        return carry

    lax.fori_loop(0, pairs, pair, 0)
    final = pairs - 1
    at = lax.rem(final, 2) * 2
    for each in add_terms([(2 * final, x, at), (2 * final + 1, y, at + 1)]):
        each()

    moves = [
        (grad.at[:, middle, middle], inner_out),
        (grad.at[:, row_a, middle], row_a_out.at[:, :, pl.ds(0, tile)]),
        (grad.at[:, row_b, middle], row_b_out.at[:, :, pl.ds(0, tile)]),
        (grad.at[:, row_a, col_b], row_a_out.at[:, :, pl.ds(tile, HALF)]),
        (grad.at[:, row_b, col_b], row_b_out.at[:, :, pl.ds(tile, HALF)]),
        (grad.at[:, middle, col_a], col_a_out),
        (grad.at[:, middle, col_b], col_b_out),
        (grad.at[:, row_a, col_a], corner_out.at[0]),
        (grad.at[:, row_b, col_a], corner_out.at[1]),
    ]
    me = side_ref[2]
    half_rows = probe_keep.shape[0] - 8
    height = 2 * half_rows // pieces
    per_square = W // height
    for piece in range(pieces):
        which = piece ^ me
        square, block = which // per_square, lax.rem(which, per_square)
        source = probe_grad.at[
            square // MODES, lax.rem(square, MODES), pl.ds(pl.multiple_of(block * height, 8), height)
        ]
        target = probe_keep if piece < pieces // 2 else probe_away
        moves.append((source, target.at[pl.ds(piece % (pieces // 2) * height, height)]))
    counted[...] = jnp.full(counted.shape, count.astype(jnp.float32))
    moves += [(counted, target.at[pl.ds(half_rows, 8)]) for target in (probe_keep, probe_away)]
    for copy in run_copies(moves, sems):
        copy.wait()


def slots(sides, offsets, count, own, halos, probe, patterns, pieces):
    tile = own.shape[1]
    wide = tile + 2 * HALF
    smem = pl.BlockSpec(memory_space=pltpu.SMEM)
    anywhere = pl.BlockSpec(memory_space=pl.ANY)
    ahead, back = tables()
    square = (2 * W, 2 * W)
    buffers = [
        pltpu.VMEM(square, kind)
        for kind in (jnp.bfloat16, jnp.bfloat16, jnp.float32, jnp.bfloat16, jnp.bfloat16, jnp.float32)
    ]
    outs = [
        (MODES * W + 8, W),
        (MODES * W + 8, W),
        (2, tile, tile),
        (2, HALF, tile + HALF),
        (2, HALF, tile + HALF),
        (2, tile, HALF),
        (2, tile, HALF),
        (2, 2, HALF, HALF),
    ]
    return pl.pallas_call(
        functools.partial(slots_kernel, pieces),
        out_shape=[jax.ShapeDtypeStruct(shape, jnp.float32) for shape in outs],
        in_specs=[smem] * 3 + [pl.BlockSpec(memory_space=pltpu.HBM)] * 11,
        out_specs=[anywhere] * len(outs),
        scratch_shapes=[
            pltpu.VMEM((2, wide, wide), jnp.float32),
            pltpu.VMEM((2, wide, wide), jnp.float32),
            pltpu.VMEM((2, MODES, W, W), jnp.float32),
            pltpu.VMEM((4, 2, W, W), jnp.float32),
            *buffers,
            *buffers,
            pltpu.VMEM(probe.shape, jnp.float32),
            pltpu.VMEM(patterns.shape, patterns.dtype),
            pltpu.VMEM(square, jnp.bfloat16),
            pltpu.VMEM(square, jnp.bfloat16),
            pltpu.VMEM((8, W), jnp.float32),
            pltpu.SemaphoreType.DMA((13 + pieces,)),
        ],
        compiler_params=pltpu.CompilerParams(vmem_limit_bytes=VMEM_BYTES),
    )(sides, offsets, count, own, *halos, probe, patterns, jnp.asarray(ahead), jnp.asarray(back))


def join_kernel(
    side_ref, inner_ref, row_a_ref, row_b_ref, col_a_ref, col_b_ref, out_ref
):
    row_a, row_b, col_a, col_b = inner_edges(side_ref, inner_ref.shape[1])
    out_ref[...] = inner_ref[...]
    tile = inner_ref.shape[1]
    out_ref[:, row_a, :] += row_a_ref[:, :, :tile]
    out_ref[:, row_b, :] += row_b_ref[:, :, :tile]
    out_ref[:, :, col_a] += col_a_ref[...]
    out_ref[:, :, col_b] += col_b_ref[...]


def join(sides, inner, *terms):
    vmem = pl.BlockSpec(memory_space=pltpu.VMEM)
    return pl.pallas_call(
        join_kernel,
        out_shape=jax.ShapeDtypeStruct(inner.shape, jnp.float32),
        in_specs=[pl.BlockSpec(memory_space=pltpu.SMEM)] + [vmem] * (1 + len(terms)),
        out_specs=vmem,
        compiler_params=pltpu.CompilerParams(vmem_limit_bytes=VMEM_BYTES),
    )(sides, inner, *terms)


def cut(x, start, dim):
    return lax.dynamic_slice_in_dim(x, start, HALF, axis=dim)


def add_at(strip, term, start):
    old = lax.dynamic_slice_in_dim(strip, start, term.shape[2], axis=2)
    return lax.dynamic_update_slice_in_dim(strip, old + term, start, axis=2)


def gathered(part, axis, bits):
    other = exchange(part, axis, bits)
    first = lax.axis_index(axis) // bits % 2 == 0
    return jnp.where(first, jnp.concatenate([part, other]), jnp.concatenate([other, part]))


def local(object_field, probe, positions, counts, patterns):
    tile = object_field.shape[1]
    edge = tile - HALF
    barrier = lax.optimization_barrier
    row, col = lax.axis_index("row"), lax.axis_index("col")
    live = counts[0, 0]
    halvings = [
        (axis, 1 << i)
        for axis in ("col", "row")
        for i in range(lax.axis_size(axis).bit_length() - 1)
    ]
    halvings, last = halvings[:-1], halvings[-1]
    pieces = 1 << len(halvings)
    mine = 0
    for axis, bits in halvings:
        mine = 2 * mine + lax.axis_index(axis) // bits % 2
    sides = jnp.stack([row % 2, col % 2, mine]).astype(jnp.int32)

    row_a = swap(cut(object_field, (1 - row % 2) * edge, 1), "row", 0)
    row_b = swap(cut(object_field, row % 2 * edge, 1), "row", 1)
    col_a = swap(cut(object_field, (1 - col % 2) * edge, 2), "col", 0)
    col_b = swap(cut(object_field, col % 2 * edge, 2), "col", 1)
    corner_a = jnp.stack([cut(strip, (1 - col % 2) * edge, 2) for strip in (row_a, row_b)])
    corner_b = jnp.stack([cut(strip, col % 2 * edge, 2) for strip in (row_a, row_b)])
    corner_b = swap(corner_b, "col", 1)
    corner_a = swap(corner_a, "col", 0)

    keep, away, inner, row_a, row_b, col_a, col_b, corner = slots(
        sides,
        positions[0, 0],
        live[None],
        object_field,
        (row_a, row_b, col_a, col_b, corner_a, corner_b),
        probe,
        patterns[0, 0],
        pieces,
    )

    corner, away = barrier((swap(corner, "col", 0), away))
    away = exchange(away, *halvings[0])
    row_a = swap(add_at(row_a, corner[0], (1 - col % 2) * edge), "row", 0)
    row_b = swap(add_at(row_b, corner[1], (1 - col % 2) * edge), "row", 1)
    keep = keep + away
    col_a = swap(col_a, "col", 0)
    for index, (axis, bits) in enumerate(halvings[1:]):
        half = (keep.shape[0] - 8) // 2
        keep = jnp.concatenate([keep[:half], keep[-8:]]) + exchange(keep[half:], axis, bits)
        if index == 0:
            keep, row_a, row_b, col_a, col_b = barrier((keep, row_a, row_b, col_a, col_b))
            top, bottom = [
                jnp.where(row % 2 == 1, first, second)[:, :, tile:]
                for first, second in ((row_a, row_b), (row_b, row_a))
            ]
            blank = jnp.zeros((2, tile - 2 * HALF, HALF), jnp.float32)
            col_b = swap(col_b + jnp.concatenate([top, blank, bottom], axis=1), "col", 1)
    keep = keep + exchange(keep, *last)
    part = keep[:-8] / keep[-8:-7]
    for axis, bits in reversed(halvings):
        if bits == 1 and axis == "row":
            part = gathered(part, axis, bits)
            part, col_b = barrier((part, col_b))
        elif (axis, bits) != halvings[0]:
            part = gathered(part, axis, bits)
    result = join(sides, inner, row_a, row_b, col_a, col_b)
    part, result = barrier((part, result))
    whole = gathered(part, *halvings[0])
    return result, whole.reshape(probe.shape)


def solution(mesh):
    placed = (
        P(None, ("groups", "row"), "col"),
        P(None, "groups", None, None),
        P(("groups", "row"), "col", None, None),
        P(("groups", "row"), "col"),
        P(("groups", "row"), "col", None, None, None),
    )
    return jax.shard_map(
        local,
        mesh=mesh,
        in_specs=placed,
        out_specs=(P(None, ("groups", "row"), "col"), P(None, "groups", None, None)),
        check_vma=False,
    )
```

```python
import functools
import math

import jax
import jax.numpy as jnp
import ml_dtypes
import numpy as np
from jax import lax
from jax.experimental import pallas as pl
from jax.experimental.pallas import tpu as pltpu
from jax.sharding import PartitionSpec as P

W = 256
MODES = 2
KMAX = 8
HALF = W // 2
LANES = 128
GROUPS = W // 8
VMEM_BYTES = 50 * 1024 * 1024


def tables():
    counter = np.arange(W)
    phases = (counter[:, None] * counter[None, :] % W).astype(np.float32)
    angles = (np.float32(2.0 * math.pi / W) * phases).astype(np.float32)
    scaling = np.float32(1.0 / math.sqrt(W))
    cosine = (np.cos(angles) * scaling).astype(ml_dtypes.bfloat16)
    sine = (np.sin(angles) * scaling).astype(ml_dtypes.bfloat16)
    ahead = np.block([[cosine, -sine], [sine, cosine]])
    back = np.block([[cosine, sine], [-sine, cosine]])
    return ahead, back


def side_pairs(size, parity):
    pairs = [(i, i + 1) for i in range(parity, size - 1, 2)]
    return pairs + [(j, i) for i, j in pairs]


def swap(x, axis, parity):
    return lax.ppermute(x, axis, side_pairs(lax.axis_size(axis), parity))


def exchange(x, axis, bits):
    size = lax.axis_size(axis)
    return lax.ppermute(x, axis, [(i, i ^ bits) for i in range(size)])


def edges(side_ref, tile):
    far_edge = tile + HALF
    row_odd, col_odd = side_ref[0], side_ref[1]
    row_a = pl.multiple_of((1 - row_odd) * far_edge, LANES)
    row_b = pl.multiple_of(row_odd * far_edge, LANES)
    col_a = pl.multiple_of((1 - col_odd) * far_edge, LANES)
    col_b = pl.multiple_of(col_odd * far_edge, LANES)
    return [pl.ds(start, HALF) for start in (row_a, row_b, col_a, col_b)]


def inner_edges(side_ref, tile):
    edge = tile - HALF
    row_odd, col_odd = side_ref[0], side_ref[1]
    row_a = pl.multiple_of((1 - row_odd) * edge, LANES)
    row_b = pl.multiple_of(row_odd * edge, LANES)
    col_a = pl.multiple_of((1 - col_odd) * edge, LANES)
    col_b = pl.multiple_of(col_odd * edge, LANES)
    return [pl.ds(start, HALF) for start in (row_a, row_b, col_a, col_b)]


def run_copies(moves, sems):
    copies = [
        pltpu.make_async_copy(source, target, sems.at[index])
        for index, (source, target) in enumerate(moves)
    ]
    for copy in copies:
        copy.start()
    return copies


def merge(first, second):
    order = [((i + 0.5) / len(first), 0, step) for i, step in enumerate(first)]
    order += [((i + 0.5) / len(second), 1, step) for i, step in enumerate(second)]
    for _, _, step in sorted(order, key=lambda entry: entry[:2]):
        step()


def slots_kernel(
    pieces,
    side_ref,
    offsets_ref,
    count_ref,
    own_ref,
    row_a_ref,
    row_b_ref,
    col_a_ref,
    col_b_ref,
    corner_a_ref,
    corner_b_ref,
    probe_in,
    patterns_in,
    ahead_in,
    back_in,
    probe_keep,
    probe_away,
    inner_out,
    row_a_out,
    row_b_out,
    col_a_out,
    col_b_out,
    corner_out,
    padded,
    grad,
    probe_grad,
    windows,
    *rest,
):
    sets = (rest[0:6], rest[6:12])
    probe_ref, patterns_ref, ahead_ref, back_ref, counted, sems = rest[12:]
    tile = own_ref.shape[1]
    row_a, row_b, col_a, col_b = edges(side_ref, tile)
    middle = pl.ds(HALF, tile)
    copies = run_copies(
        [
            (own_ref, padded.at[:, middle, middle]),
            (row_a_ref, padded.at[:, row_a, middle]),
            (row_b_ref, padded.at[:, row_b, middle]),
            (col_a_ref, padded.at[:, middle, col_a]),
            (col_b_ref, padded.at[:, middle, col_b]),
            (corner_a_ref.at[0], padded.at[:, row_a, col_a]),
            (corner_a_ref.at[1], padded.at[:, row_b, col_a]),
            (corner_b_ref.at[0], padded.at[:, row_a, col_b]),
            (corner_b_ref.at[1], padded.at[:, row_b, col_b]),
            (probe_in, probe_ref),
            (patterns_in, patterns_ref),
            (ahead_in, ahead_ref),
            (back_in, back_ref),
        ],
        sems,
    )
    grad[...] = jnp.zeros_like(grad)
    probe_grad[...] = jnp.zeros_like(probe_grad)
    for copy in copies[:-3]:
        copy.wait()
    lane = lax.broadcasted_iota(jnp.int32, (8, LANES), 1)
    sub = lax.broadcasted_iota(jnp.int32, (8, LANES), 0)
    zero = jnp.zeros((8, LANES), jnp.float32)
    batch = 4
    step = 8 * batch

    def place(k):
        row, column = offsets_ref[0, k], offsets_ref[1, k]
        row_base = pl.multiple_of(row // 8 * 8, 8)
        col_base = pl.multiple_of(column // LANES * LANES, LANES)
        return row_base, row - row_base, col_base, column - col_base

    def make_wave(k, buffers, w):
        wave = buffers[0]
        row_base, row_shift, col_base, col_shift = place(k)
        in_lane, in_sub = lane < LANES - col_shift, sub < 8 - row_shift
        lane_turn = lax.rem(LANES - col_shift, LANES)
        sub_turn = lax.rem(8 - row_shift, 8)
        before = {}

        def turned(plane, group):
            rows = pl.ds(row_base + 8 * group, 8)
            parts = [
                pltpu.roll(padded[plane, rows, pl.ds(col_base + LANES * j, LANES)], lane_turn, 1)
                for j in range(3)
            ]
            return [
                pltpu.roll(jnp.where(in_lane, parts[j], parts[j + 1]), sub_turn, 0)
                for j in range(2)
            ]

        def some_rows(first):
            if first == 0:
                for plane in range(2):
                    before[plane] = turned(plane, 0)
            pieces = [[], []]
            for group in range(first, first + batch):
                for plane in range(2):
                    after = turned(plane, group + 1)
                    value = jnp.concatenate(
                        [jnp.where(in_sub, b, a) for b, a in zip(before[plane], after)], axis=1
                    )
                    windows[w, plane, 8 * group : 8 * group + 8, :] = value
                    pieces[plane].append(value)
                    before[plane] = after
            object_real, object_imag = [jnp.concatenate(piece, axis=0) for piece in pieces]
            start = 8 * first
            rows = slice(start, start + step)
            for m in range(MODES):
                probe_real, probe_imag = probe_ref[0, m, rows, :], probe_ref[1, m, rows, :]
                into = slice(m * W + start, m * W + start + step)
                wave[into, :W] = (probe_real * object_real - probe_imag * object_imag).astype(
                    jnp.bfloat16
                )
                wave[into, W:] = (probe_real * object_imag + probe_imag * object_real).astype(
                    jnp.bfloat16
                )

        return [functools.partial(some_rows, first) for first in range(0, GROUPS, batch)]

    def right(source, table, target):
        product = jnp.dot(
            source[...], table[...], preferred_element_type=jnp.float32
        ).astype(jnp.bfloat16)
        for m in range(MODES):
            rows = slice(m * W, m * W + W)
            target[:W, rows] = product[rows, :W]
            target[W:, rows] = product[rows, W:]

    def left(source, table, target, m):
        columns = slice(m * W, m * W + W)
        target[:, columns] = jnp.dot(
            table[...], source[:, columns], preferred_element_type=jnp.float32
        )

    def ahead_right(buffers):
        return functools.partial(right, buffers[0], ahead_ref, buffers[1])

    def ahead_left(buffers, m):
        return functools.partial(left, buffers[1], back_ref, buffers[2], m)

    def back_right(buffers):
        return functools.partial(right, buffers[3], back_ref, buffers[4])

    def back_left(buffers, m):
        return functools.partial(left, buffers[4], ahead_ref, buffers[5], m)

    def weigh(k, live, buffers):
        far, weighted = buffers[2], buffers[3]

        def some_rows(start):
            rows = slice(start, start + step)
            imag_rows = slice(W + start, W + start + step)
            reals = [far[rows, m * W : m * W + W] for m in range(MODES)]
            imags = [far[imag_rows, m * W : m * W + W] for m in range(MODES)]
            intensity = sum(r * r + i * i for r, i in zip(reals, imags))
            residual = intensity - patterns_ref[k, rows, :].astype(jnp.float32)
            if live is not None:
                residual = residual * live
            for m in range(MODES):
                into = slice(m * W + start, m * W + start + step)
                weighted[into, :W] = (residual * reals[m]).astype(jnp.bfloat16)
                weighted[into, W:] = (residual * imags[m]).astype(jnp.bfloat16)

        return [functools.partial(some_rows, start) for start in range(0, W, step)]

    def add_terms(members):
        info = []
        for k, _, _ in members:
            row_base, row_shift, col_base, col_shift = place(k)
            info.append(
                (row_base, row_shift, col_base, col_shift, lane >= col_shift, sub >= row_shift)
            )

        def terms(start, low):
            rows = slice(start, start + 8)
            imag_rows = slice(W + start, W + start + 8)
            columns = slice(low, low + LANES)
            turned = []
            totals = [[None, None] for _ in range(MODES)]
            probes = [[probe_ref[plane, m, rows, columns] for plane in range(2)] for m in range(MODES)]
            for (_, buffers, w), (_, row_shift, _, col_shift, _, _) in zip(members, info):
                chi = buffers[5]
                object_real, object_imag = windows[w, 0, rows, columns], windows[w, 1, rows, columns]
                sums = [None, None]
                for m in range(MODES):
                    at = slice(m * W + low, m * W + low + LANES)
                    chi_real, chi_imag = chi[rows, at], chi[imag_rows, at]
                    probe_real, probe_imag = probes[m]
                    mine = (
                        object_real * chi_real + object_imag * chi_imag,
                        object_real * chi_imag - object_imag * chi_real,
                    )
                    more = (
                        probe_real * chi_real + probe_imag * chi_imag,
                        probe_real * chi_imag - probe_imag * chi_real,
                    )
                    for plane in range(2):
                        total = totals[m][plane]
                        totals[m][plane] = mine[plane] if total is None else total + mine[plane]
                        total = sums[plane]
                        sums[plane] = more[plane] if total is None else total + more[plane]
                turned.append(
                    [pltpu.roll(pltpu.roll(value, col_shift, 1), row_shift, 0) for value in sums]
                )
            for m in range(MODES):
                for plane in range(2):
                    probe_grad[plane, m, rows, columns] += totals[m][plane]
            return turned

        nothing = [[zero, zero] for _ in members]
        before = [nothing, nothing]

        def some_groups(first):
            groups = range(first, min(first + batch, GROUPS + 1))
            news = []
            for group in groups:
                if group < GROUPS:
                    news.append([terms(8 * group, 0), terms(8 * group, LANES)])
                else:
                    news.append([nothing, nothing])
            for q, (row_base, _, col_base, _, from_lane, from_sub) in enumerate(info):
                adds = []
                last = [before[0][q], before[1][q]]
                for group, new in zip(groups, news):
                    rows = pl.ds(row_base + 8 * group, 8)
                    for plane in range(2):
                        low, high = [
                            jnp.where(from_sub, new[half][q][plane], last[half][plane])
                            for half in range(2)
                        ]
                        values = (
                            jnp.where(from_lane, low, 0.0),
                            jnp.where(from_lane, high, low),
                            jnp.where(from_lane, 0.0, high),
                        )
                        for j, value in enumerate(values):
                            adds.append((plane, rows, pl.ds(col_base + LANES * j, LANES), value))
                    last = [new[0][q], new[1][q]]
                olds = [grad[plane, rows, columns] for plane, rows, columns, _ in adds]
                for (plane, rows, columns, value), old in zip(adds, olds):
                    grad[plane, rows, columns] = old + value
            before[:] = news[-1]

        return [functools.partial(some_groups, first) for first in range(0, GROUPS + 1, batch)]

    count = count_ref[0]
    pairs = (count + 1) // 2
    x, y = sets
    for each in make_wave(0, x, 0) + make_wave(1, y, 1):
        each()
    for copy in copies[-3:]:
        copy.wait()

    def pair(index, carry, opening=False):
        now = (2 * index, 2 * index + 1)
        past = [jnp.maximum(k - 2, 0) for k in now]
        later = [jnp.minimum(k + 2, KMAX - 1) for k in now]
        other = 2 - lax.rem(index, 2) * 2
        live = (now[1] < count).astype(jnp.float32)
        adds = [] if opening else add_terms([(past[0], x, other), (past[1], y, other + 1)])
        some = len(adds) * 2 // 3
        merge(
            [ahead_right(b) for b in sets]
            + [ahead_left(x, m) for m in range(MODES)],
            adds[:some],
        )
        merge([ahead_left(y, m) for m in range(MODES)], adds[some:] + weigh(now[0], None, x))
        merge([back_right(x)], weigh(now[1], live, y))
        merge(
            [back_right(y)]
            + [back_left(b, m) for b in sets for m in range(MODES)],
            make_wave(later[0], x, other) + make_wave(later[1], y, other + 1),
        )
        return carry

    pair(0, 0, opening=True)
    lax.fori_loop(1, pairs, pair, 0)
    final = pairs - 1
    at = lax.rem(final, 2) * 2
    for each in add_terms([(2 * final, x, at), (2 * final + 1, y, at + 1)]):
        each()

    moves = [
        (grad.at[:, middle, middle], inner_out),
        (grad.at[:, row_a, middle], row_a_out.at[:, :, pl.ds(0, tile)]),
        (grad.at[:, row_b, middle], row_b_out.at[:, :, pl.ds(0, tile)]),
        (grad.at[:, row_a, col_b], row_a_out.at[:, :, pl.ds(tile, HALF)]),
        (grad.at[:, row_b, col_b], row_b_out.at[:, :, pl.ds(tile, HALF)]),
        (grad.at[:, middle, col_a], col_a_out),
        (grad.at[:, middle, col_b], col_b_out),
        (grad.at[:, row_a, col_a], corner_out.at[0]),
        (grad.at[:, row_b, col_a], corner_out.at[1]),
    ]
    me = side_ref[2]
    half_rows = probe_keep.shape[0] - 8
    height = 2 * half_rows // pieces
    per_square = W // height
    for piece in range(pieces):
        which = piece ^ me
        square, block = which // per_square, lax.rem(which, per_square)
        source = probe_grad.at[
            square // MODES, lax.rem(square, MODES), pl.ds(pl.multiple_of(block * height, 8), height)
        ]
        target = probe_keep if piece < pieces // 2 else probe_away
        moves.append((source, target.at[pl.ds(piece % (pieces // 2) * height, height)]))
    counted[...] = jnp.full(counted.shape, count.astype(jnp.float32))
    moves += [(counted, target.at[pl.ds(half_rows, 8)]) for target in (probe_keep, probe_away)]
    for copy in run_copies(moves, sems):
        copy.wait()


def slots(sides, offsets, count, own, halos, probe, patterns, pieces):
    tile = own.shape[1]
    wide = tile + 2 * HALF
    smem = pl.BlockSpec(memory_space=pltpu.SMEM)
    anywhere = pl.BlockSpec(memory_space=pl.ANY)
    ahead, back = tables()
    square = (2 * W, 2 * W)
    buffers = [
        pltpu.VMEM(square, kind)
        for kind in (jnp.bfloat16, jnp.bfloat16, jnp.float32, jnp.bfloat16, jnp.bfloat16, jnp.float32)
    ]
    outs = [
        (MODES * W + 8, W),
        (MODES * W + 8, W),
        (2, tile, tile),
        (2, HALF, tile + HALF),
        (2, HALF, tile + HALF),
        (2, tile, HALF),
        (2, tile, HALF),
        (2, 2, HALF, HALF),
    ]
    return pl.pallas_call(
        functools.partial(slots_kernel, pieces),
        out_shape=[jax.ShapeDtypeStruct(shape, jnp.float32) for shape in outs],
        in_specs=[smem] * 3 + [pl.BlockSpec(memory_space=pltpu.HBM)] * 11,
        out_specs=[anywhere] * len(outs),
        scratch_shapes=[
            pltpu.VMEM((2, wide, wide), jnp.float32),
            pltpu.VMEM((2, wide, wide), jnp.float32),
            pltpu.VMEM((2, MODES, W, W), jnp.float32),
            pltpu.VMEM((4, 2, W, W), jnp.float32),
            *buffers,
            *buffers,
            pltpu.VMEM(probe.shape, jnp.float32),
            pltpu.VMEM(patterns.shape, patterns.dtype),
            pltpu.VMEM(square, jnp.bfloat16),
            pltpu.VMEM(square, jnp.bfloat16),
            pltpu.VMEM((8, W), jnp.float32),
            pltpu.SemaphoreType.DMA((13 + pieces,)),
        ],
        compiler_params=pltpu.CompilerParams(vmem_limit_bytes=VMEM_BYTES),
    )(sides, offsets, count, own, *halos, probe, patterns, jnp.asarray(ahead), jnp.asarray(back))


def join_kernel(
    side_ref, inner_ref, row_a_ref, row_b_ref, col_a_ref, col_b_ref, out_ref
):
    row_a, row_b, col_a, col_b = inner_edges(side_ref, inner_ref.shape[1])
    out_ref[...] = inner_ref[...]
    tile = inner_ref.shape[1]
    out_ref[:, row_a, :] += row_a_ref[:, :, :tile]
    out_ref[:, row_b, :] += row_b_ref[:, :, :tile]
    out_ref[:, :, col_a] += col_a_ref[...]
    out_ref[:, :, col_b] += col_b_ref[...]


def join(sides, inner, *terms):
    vmem = pl.BlockSpec(memory_space=pltpu.VMEM)
    return pl.pallas_call(
        join_kernel,
        out_shape=jax.ShapeDtypeStruct(inner.shape, jnp.float32),
        in_specs=[pl.BlockSpec(memory_space=pltpu.SMEM)] + [vmem] * (1 + len(terms)),
        out_specs=vmem,
        compiler_params=pltpu.CompilerParams(vmem_limit_bytes=VMEM_BYTES),
    )(sides, inner, *terms)


def cut(x, start, dim):
    return lax.dynamic_slice_in_dim(x, start, HALF, axis=dim)


def add_at(strip, term, start):
    old = lax.dynamic_slice_in_dim(strip, start, term.shape[2], axis=2)
    return lax.dynamic_update_slice_in_dim(strip, old + term, start, axis=2)


def gathered(part, axis, bits):
    other = exchange(part, axis, bits)
    first = lax.axis_index(axis) // bits % 2 == 0
    return jnp.where(first, jnp.concatenate([part, other]), jnp.concatenate([other, part]))


def local(object_field, probe, positions, counts, patterns):
    tile = object_field.shape[1]
    edge = tile - HALF
    barrier = lax.optimization_barrier
    row, col = lax.axis_index("row"), lax.axis_index("col")
    live = counts[0, 0]
    halvings = [
        (axis, 1 << i)
        for axis in ("col", "row")
        for i in range(lax.axis_size(axis).bit_length() - 1)
    ]
    halvings, last = halvings[:-1], halvings[-1]
    pieces = 1 << len(halvings)
    mine = 0
    for axis, bits in halvings:
        mine = 2 * mine + lax.axis_index(axis) // bits % 2
    sides = jnp.stack([row % 2, col % 2, mine]).astype(jnp.int32)

    row_a = swap(cut(object_field, (1 - row % 2) * edge, 1), "row", 0)
    row_b = swap(cut(object_field, row % 2 * edge, 1), "row", 1)
    col_a = swap(cut(object_field, (1 - col % 2) * edge, 2), "col", 0)
    col_b = swap(cut(object_field, col % 2 * edge, 2), "col", 1)
    corner_a = jnp.stack([cut(strip, (1 - col % 2) * edge, 2) for strip in (row_a, row_b)])
    corner_b = jnp.stack([cut(strip, col % 2 * edge, 2) for strip in (row_a, row_b)])
    corner_b = swap(corner_b, "col", 1)
    corner_a = swap(corner_a, "col", 0)

    keep, away, inner, row_a, row_b, col_a, col_b, corner = slots(
        sides,
        positions[0, 0],
        live[None],
        object_field,
        (row_a, row_b, col_a, col_b, corner_a, corner_b),
        probe,
        patterns[0, 0],
        pieces,
    )

    corner, away = barrier((swap(corner, "col", 0), away))
    away = exchange(away, *halvings[0])
    row_a = swap(add_at(row_a, corner[0], (1 - col % 2) * edge), "row", 0)
    row_b = swap(add_at(row_b, corner[1], (1 - col % 2) * edge), "row", 1)
    keep = keep + away
    col_a = swap(col_a, "col", 0)
    for index, (axis, bits) in enumerate(halvings[1:]):
        half = (keep.shape[0] - 8) // 2
        keep = jnp.concatenate([keep[:half], keep[-8:]]) + exchange(keep[half:], axis, bits)
        if index == 0:
            keep, row_a, row_b, col_a, col_b = barrier((keep, row_a, row_b, col_a, col_b))
            top, bottom = [
                jnp.where(row % 2 == 1, first, second)[:, :, tile:]
                for first, second in ((row_a, row_b), (row_b, row_a))
            ]
            blank = jnp.zeros((2, tile - 2 * HALF, HALF), jnp.float32)
            col_b = swap(col_b + jnp.concatenate([top, blank, bottom], axis=1), "col", 1)
    keep = keep + exchange(keep, *last)
    part = keep[:-8] / keep[-8:-7]
    for axis, bits in reversed(halvings):
        if bits == 1 and axis == "row":
            part = gathered(part, axis, bits)
            part, col_b = barrier((part, col_b))
        elif (axis, bits) != halvings[0]:
            part = gathered(part, axis, bits)
    result = join(sides, inner, row_a, row_b, col_a, col_b)
    part, result = barrier((part, result))
    whole = gathered(part, *halvings[0])
    return result, whole.reshape(probe.shape)


def solution(mesh):
    placed = (
        P(None, ("groups", "row"), "col"),
        P(None, "groups", None, None),
        P(("groups", "row"), "col", None, None),
        P(("groups", "row"), "col"),
        P(("groups", "row"), "col", None, None, None),
    )
    return jax.shard_map(
        local,
        mesh=mesh,
        in_specs=placed,
        out_specs=(P(None, ("groups", "row"), "col"), P(None, "groups", None, None)),
        check_vma=False,
    )
```
